32 devices in a mesh: hi: 8 (over y, x, core), lo: 4 (over z).
Axes of the slice: x: 2, y: 2, z: 4, core: 2. Of those that a mesh axis runs over, the one named last changes fastest.
Arguments:
- design: float32 [16, 524288], P(None, ('hi', 'lo')), may hold values from -24 to 24
- signs: int32 [524288], P(('hi', 'lo')), may hold values from -1 to 1, as said below
- samples: int32 [1024], replicated, may hold values from 0 to 524287, as said below
Outputs:
- sampled: float32 [16, 1024], P(None, ('hi', 'lo'))
- gram: float32 [16, 16], replicated
The draws below stay inside these ranges and needn't reach their ends.
Inputs may be any that keep to these rules, and one draw needn't show every extreme that they name: `signs`: each is +1 or -1. `samples`: non-decreasing; the first is 0 and the last is 524287; an index may repeat.
All inputs are finite; a program needn't handle non-finite values.
Results may differ from the reference program's by a relative error of at most 0.000073.
Values sent between devices are 32-bit elements; how exact they have to be, the bound alone decides.
A program may use at most 64 MiB of HBM per device.

```python
import math
import jax
import jax.numpy as jnp
from jax import lax

COLS = 16
LOG_DEV = 14
LEN_DEV = 16384
TOTAL_ROWS = 524288
SAMPLES = 1024
N_HI = 8
N_LO = 4


def draw_design(key, part):
    key = jax.random.fold_in(key, 11)
    key_scale, key_noise, key_common = jax.random.split(key, 3)
    column_scale = jnp.exp(jax.random.uniform(key_scale, (COLS, 1), jnp.float32, jnp.log(0.3), jnp.log(3.0)))
    noise = jnp.clip(jax.random.normal(key_noise, (COLS, TOTAL_ROWS), jnp.float32), -5.0, 5.0)
    shared = jnp.clip(jax.random.normal(key_common, (1, TOTAL_ROWS), jnp.float32), -5.0, 5.0)
    values = column_scale * (noise + 0.6 * shared)
    return values.astype(jnp.float32)


def draw_signs(key, part):
    key = jax.random.fold_in(key, 23)
    return (2 * jax.random.randint(key, (TOTAL_ROWS,), 0, 2) - 1).astype(jnp.int32)


def draw_samples(key, part):
    key = jax.random.fold_in(key, 37)
    picks = jax.random.randint(key, (SAMPLES,), 0, TOTAL_ROWS).astype(jnp.int32)
    picks = picks.at[0].set(0).at[SAMPLES - 1].set(TOTAL_ROWS - 1)
    return jnp.sort(picks).astype(jnp.int32)


def setup_inputs(seed: int = 0) -> dict:
    splits = jax.random.split(jax.random.key(seed), 4)
    design = draw_design(jax.random.fold_in(splits[3], 71), 0)
    signs = draw_signs(jax.random.fold_in(splits[3], 71), 0)
    samples = draw_samples(jax.random.fold_in(splits[3], 71), 0)
    return dict(design=design, signs=signs, samples=samples)


def hadamard_table(count):
    positions = jnp.arange(count, dtype=jnp.int32)
    common = jnp.bitwise_and(positions[:, None], positions[None, :])
    parity = jnp.zeros((count, count), jnp.int32)
    for bit_number in range(count.bit_length() - 1):
        parity = parity + jnp.bitwise_and(jnp.right_shift(common, bit_number), 1)
    return (1 - 2 * (parity % 2)).astype(jnp.float32)

def reference(design, signs, samples):
    blocks = N_HI * N_LO
    low_size = 2 ** (LOG_DEV // 2)
    high_size = LEN_DEV // low_size
    table_low = hadamard_table(low_size)
    table_high = hadamard_table(high_size)
    sample_block = (samples // LEN_DEV).astype(jnp.int32)
    within = (samples % LEN_DEV).astype(jnp.int32)
    block_ids = jnp.arange(blocks, dtype=jnp.int32)
    common = jnp.bitwise_and(block_ids[:, None], sample_block[None, :])
    parity = jnp.zeros((blocks, SAMPLES), jnp.int32)
    for bit_number in range(blocks.bit_length() - 1):
        parity = parity + jnp.bitwise_and(jnp.right_shift(common, bit_number), 1)
    sign_table = (1 - 2 * (parity % 2)).astype(jnp.float32)
    sign_values = signs.astype(jnp.float32)

    def one_column(column):
        flipped = (column * sign_values).reshape(blocks, high_size, low_size)
        section = jnp.einsum('bpq,qr->bpr', flipped, table_low, precision=lax.Precision.HIGHEST)
        section = jnp.einsum('bpq,pk->bkq', section, table_high, precision=lax.Precision.HIGHEST)
        local = section.reshape(blocks, LEN_DEV)
        picked = jnp.take(local, within, axis=1)
        return lax.optimization_barrier(jnp.sum(picked * sign_table, axis=0))
    summed = lax.map(one_column, design)
    sampled = summed * (1.0 / math.sqrt(TOTAL_ROWS))
    gram = jnp.dot(sampled, sampled.T, precision=lax.Precision.HIGHEST) / SAMPLES
    return (sampled, gram)
```

```python
import functools
import math

import jax
import jax.numpy as jnp
from jax import lax
from jax.experimental import pallas as pl
from jax.experimental.pallas import tpu as pltpu
from jax.sharding import PartitionSpec as P

LANES = 128
LOW_BITS = 8
LOADS = 4


def bit_sign(values, bit):
    return (1 - 2 * jnp.bitwise_and(jnp.right_shift(values, bit), 1)).astype(jnp.float32)


def parity_sign(values, bits):
    step = 1
    while step < bits:
        values = jnp.bitwise_xor(values, jnp.right_shift(values, step))
        step *= 2
    return bit_sign(values, 0)


def low_table(rows):
    width = rows.shape[1]
    octet = lax.broadcasted_iota(jnp.int32, (8, width), 0)
    table = parity_sign(jnp.bitwise_and(octet, jnp.broadcast_to(rows, (8, width))), 3)
    blocks = [table]
    for bit in range(3, LOW_BITS):
        sign = jnp.broadcast_to(bit_sign(rows, bit), (8, width))
        blocks = blocks + [block * sign for block in blocks]
    return jnp.concatenate(blocks, axis=0).astype(jnp.bfloat16)


def sketch_kernel(
    sizes,
    design_hbm,
    signs_hbm,
    samples_ref,
    sampled_ref,
    gram_ref,
    design,
    signs,
    split,
    term,
    landed,
    part,
    grams,
    load_sem,
    sign_sem,
    send_hi,
    recv_hi,
    send_lo,
    recv_lo,
    send_gram,
    recv_gram,
):
    upper, lower, group, length, count = sizes
    columns = design.shape[0]
    low = 2**LOW_BITS
    high = length // low
    high_bits = high.bit_length() - 1
    length_bits = length.bit_length() - 1
    device_bits = (upper * lower).bit_length() - 1
    my_hi = lax.axis_index("hi")
    my_lo = lax.axis_index("lo")
    device = my_hi * lower + my_lo

    sign_load = pltpu.make_async_copy(signs_hbm, signs, sign_sem)
    sign_load.start()
    piece = length // LOADS
    loads = []
    for number in range(LOADS):
        here = pl.ds(number * piece, piece)
        loads.append(
            pltpu.make_async_copy(design_hbm.at[:, here], design.at[:, here], load_sem.at[number])
        )
        loads[-1].start()

    barrier = pltpu.get_barrier_semaphore()
    for step in range(1, upper):
        peer = lax.rem(my_hi + step, upper)
        pl.semaphore_signal(
            barrier, inc=1, device_id=(peer, my_lo), device_id_type=pl.DeviceIdType.MESH
        )
    for step in range(1, lower):
        peer = lax.rem(my_lo + step, lower)
        pl.semaphore_signal(
            barrier, inc=1, device_id=(my_hi, peer), device_id_type=pl.DeviceIdType.MESH
        )

    sign_load.wait()
    for number in range(LOADS):
        loads[number].wait()
        for block in range(number * high // LOADS, (number + 1) * high // LOADS):
            for half in range(low // LANES):
                lane = block * (low // LANES) + half
                value = design[:, lane * LANES : (lane + 1) * LANES] * signs[
                    lane : lane + 1, :
                ].astype(jnp.float32)
                top = value.astype(jnp.bfloat16)
                rest = (value - top.astype(jnp.float32)).astype(jnp.bfloat16)
                rows = slice(block * columns, (block + 1) * columns)
                split[rows, half * LANES : (half + 1) * LANES] = top
                split[rows, low + half * LANES : low + (half + 1) * LANES] = rest

    tiles = group // LANES
    per_chunk = max(1, 2 // tiles)
    chunks = upper // per_chunk
    width = per_chunk * group

    def to_hi(step):
        peer = lax.rem(my_hi + step, upper)
        return pltpu.make_async_remote_copy(
            src_ref=term.at[step - 1],
            dst_ref=landed.at[step - 1],
            send_sem=send_hi.at[step - 1],
            recv_sem=recv_hi.at[step - 1],
            device_id=(peer, my_lo),
            device_id_type=pl.DeviceIdType.MESH,
        )

    def chunk_term(chunk):
        rows = []
        for unit in range(per_chunk):
            target = lax.rem(my_hi + chunk * per_chunk + unit + 1, upper)
            for tile in range(tiles):
                rows.append(samples_ref[pl.ds(target * tiles + tile, 1), :])
        rows = jnp.concatenate(rows, axis=1)
        table = low_table(rows)
        table = jnp.concatenate([table, table], axis=0)
        product = jnp.dot(split[...], table, preferred_element_type=jnp.float32)
        blocks = [product[p * columns : (p + 1) * columns] for p in range(high)]
        for bit in range(high_bits):
            sign = jnp.broadcast_to(bit_sign(rows, LOW_BITS + bit), (columns, width))
            blocks = [blocks[2 * i] + sign * blocks[2 * i + 1] for i in range(len(blocks) // 2)]
        owner = jnp.bitwise_and(jnp.right_shift(rows, length_bits), device)
        total = blocks[0] * parity_sign(owner, device_bits)
        for unit in range(per_chunk):
            term[chunk * per_chunk + unit] = total[:, unit * group : (unit + 1) * group]

    def send_chunk(chunk):
        for unit in range(per_chunk):
            step = chunk * per_chunk + unit + 1
            to_hi(step).start()

    if chunks <= 4:
        for chunk in range(chunks):
            chunk_term(chunk)
            if chunk == 0:
                pl.semaphore_wait(barrier, upper + lower - 2)
            for unit in range(per_chunk):
                step = chunk * per_chunk + unit + 1
                if step < upper:
                    to_hi(step).start()
    else:
        pl.semaphore_wait(barrier, upper + lower - 2)

        @pl.loop(0, chunks)
        def _(chunk):
            chunk_term(chunk)
            for unit in range(per_chunk):
                step = chunk * per_chunk + unit + 1

                @pl.when(step < upper)
                def _():
                    to_hi(step).start()

    total = term[upper - 1]
    for step in range(1, upper):
        to_hi(step).wait_recv()
        total = total + landed[step - 1]
    part[my_lo] = total

    def to_lo(step):
        peer = lax.rem(my_lo + step, lower)
        return pltpu.make_async_remote_copy(
            src_ref=part.at[my_lo],
            dst_ref=part.at[my_lo],
            send_sem=send_lo.at[step - 1],
            recv_sem=recv_lo.at[step - 1],
            device_id=(my_hi, peer),
            device_id_type=pl.DeviceIdType.MESH,
        )

    for step in range(1, lower):
        to_lo(step).start()
    for step in range(1, lower):
        to_lo(step).wait_recv()
    total = part[0]
    for source in range(1, lower):
        total = total + part[source]
    sampled = total * (1.0 / math.sqrt(length * upper * lower))
    sampled_ref[...] = sampled
    grams[my_hi] = lax.dot_general(
        sampled,
        sampled,
        (((1,), (1,)), ((), ())),
        precision=lax.Precision.HIGHEST,
        preferred_element_type=jnp.float32,
    )

    def to_gram(step):
        peer = lax.rem(my_hi + step, upper)
        return pltpu.make_async_remote_copy(
            src_ref=grams.at[my_hi],
            dst_ref=grams.at[my_hi],
            send_sem=send_gram.at[step - 1],
            recv_sem=recv_gram.at[step - 1],
            device_id=(peer, my_lo),
            device_id_type=pl.DeviceIdType.MESH,
        )

    for step in range(1, upper):
        to_gram(step).start()
    for step in range(1, upper):
        to_gram(step).wait_recv()
    gram = grams[0]
    for source in range(1, upper):
        gram = gram + grams[source]
    gram_ref[...] = gram * (1.0 / count)
    for step in range(1, upper):
        to_hi(step).wait_send()
        to_gram(step).wait_send()
    for step in range(1, lower):
        to_lo(step).wait_send()


def on_device(design, signs, samples):
    upper = lax.axis_size("hi")
    lower = lax.axis_size("lo")
    columns, length = design.shape
    count = samples.shape[0]
    group = count // upper
    low = 2**LOW_BITS
    high = length // low
    sampled, gram = pl.pallas_call(
        functools.partial(sketch_kernel, (upper, lower, group, length, count)),
        out_shape=(
            jax.ShapeDtypeStruct((columns, group), jnp.float32),
            jax.ShapeDtypeStruct((columns, columns), jnp.float32),
        ),
        in_specs=[
            pl.BlockSpec(memory_space=pl.ANY),
            pl.BlockSpec(memory_space=pl.ANY),
            pl.BlockSpec(memory_space=pltpu.VMEM),
        ],
        out_specs=(
            pl.BlockSpec(memory_space=pltpu.VMEM),
            pl.BlockSpec(memory_space=pltpu.VMEM),
        ),
        scratch_shapes=[
            pltpu.VMEM((columns, length), jnp.float32),
            pltpu.VMEM((length // LANES, LANES), jnp.int32),
            pltpu.VMEM((high * columns, 2 * low), jnp.bfloat16),
            pltpu.VMEM((upper, columns, group), jnp.float32),
            pltpu.VMEM((upper - 1, columns, group), jnp.float32),
            pltpu.VMEM((lower, columns, group), jnp.float32),
            pltpu.VMEM((upper, columns, columns), jnp.float32),
            pltpu.SemaphoreType.DMA((LOADS,)),
            pltpu.SemaphoreType.DMA,
            pltpu.SemaphoreType.DMA((upper - 1,)),
            pltpu.SemaphoreType.DMA((upper - 1,)),
            pltpu.SemaphoreType.DMA((lower - 1,)),
            pltpu.SemaphoreType.DMA((lower - 1,)),
            pltpu.SemaphoreType.DMA((upper - 1,)),
            pltpu.SemaphoreType.DMA((upper - 1,)),
        ],
        compiler_params=pltpu.CompilerParams(
            collective_id=0, has_side_effects=True, vmem_limit_bytes=32 * 2**20
        ),
    )(
        design,
        signs.reshape(length // LANES, LANES),
        samples.reshape(count // LANES, LANES),
    )
    own = group // lower
    sampled = lax.dynamic_slice_in_dim(sampled, lax.axis_index("lo") * own, own, axis=1)
    return sampled, gram


def solution(mesh):
    placed = (P(None, ("hi", "lo")), P(("hi", "lo")), P())
    return jax.shard_map(
        on_device,
        mesh=mesh,
        in_specs=placed,
        out_specs=(P(None, ("hi", "lo")), P()),
        check_vma=False,
    )
```

```python
import functools
import math

import jax
import jax.numpy as jnp
from jax import lax
from jax.experimental import pallas as pl
from jax.experimental.pallas import tpu as pltpu
from jax.sharding import PartitionSpec as P

LANES = 128
LOW_BITS = 8
LOADS = 4


def bit_sign(values, bit):
    return (1 - 2 * jnp.bitwise_and(jnp.right_shift(values, bit), 1)).astype(jnp.float32)


def parity_sign(values, bits):
    step = 1
    while step < bits:
        values = jnp.bitwise_xor(values, jnp.right_shift(values, step))
        step *= 2
    return bit_sign(values, 0)


def low_table(rows):
    width = rows.shape[1]
    octet = lax.broadcasted_iota(jnp.int32, (8, width), 0)
    table = parity_sign(jnp.bitwise_and(octet, jnp.broadcast_to(rows, (8, width))), 3)
    blocks = [table]
    for bit in range(3, LOW_BITS):
        sign = jnp.broadcast_to(bit_sign(rows, bit), (8, width))
        blocks = blocks + [block * sign for block in blocks]
    return jnp.concatenate(blocks, axis=0).astype(jnp.bfloat16)


def flip(index, mask, size):
    result = 0
    bit = 1
    while bit < size:
        result = result + bit * lax.rem(lax.div(index, bit) + lax.div(mask, bit), 2)
        bit *= 2
    return result


def sketch_kernel(
    sizes,
    design_hbm,
    signs_hbm,
    samples_hbm,
    packed_ref,
    design,
    signs,
    samples_ref,
    split,
    tables,
    term,
    landed,
    part,
    grams,
    load_sem,
    sign_sem,
    sample_sem,
    send_hi,
    recv_hi,
    send_lo,
    recv_lo,
    send_gram,
    recv_gram,
):
    upper, lower, group, length, count = sizes
    columns = design.shape[0]
    low = 2**LOW_BITS
    high = length // low
    high_bits = high.bit_length() - 1
    length_bits = length.bit_length() - 1
    device_bits = (upper * lower).bit_length() - 1
    my_hi = lax.axis_index("hi")
    my_lo = lax.axis_index("lo")
    device = my_hi * lower + my_lo

    sample_load = pltpu.make_async_copy(samples_hbm, samples_ref, sample_sem)
    sample_load.start()
    sign_load = pltpu.make_async_copy(signs_hbm, signs, sign_sem)
    sign_load.start()
    piece = length // LOADS
    loads = []
    for number in range(LOADS):
        here = pl.ds(number * piece, piece)
        loads.append(
            pltpu.make_async_copy(design_hbm.at[:, here], design.at[:, here], load_sem.at[number])
        )
        loads[-1].start()

    barrier = pltpu.get_barrier_semaphore()
    for step in range(upper - 1, 0, -1):
        peer = flip(my_hi, step, upper)
        pl.semaphore_signal(
            barrier, inc=1, device_id=(peer, my_lo), device_id_type=pl.DeviceIdType.MESH
        )
    for step in range(lower - 1, 0, -1):
        peer = flip(my_lo, step, lower)
        pl.semaphore_signal(
            barrier, inc=1, device_id=(my_hi, peer), device_id_type=pl.DeviceIdType.MESH
        )

    tiles = group // LANES
    per_chunk = max(1, 2 // tiles)
    chunks = upper // per_chunk
    width = per_chunk * group

    def masks_of(chunk):
        return [upper - 1 - chunk * per_chunk - unit for unit in range(per_chunk)]

    def chunk_rows(chunk):
        rows = []
        for mask in masks_of(chunk):
            target = flip(my_hi, mask, upper)
            for tile in range(tiles):
                rows.append(samples_ref[pl.ds(target * tiles + tile, 1), :])
        return jnp.concatenate(rows, axis=1)

    def to_hi(mask):
        return pltpu.make_async_remote_copy(
            src_ref=term.at[mask],
            dst_ref=landed.at[mask - 1],
            send_sem=send_hi.at[mask - 1],
            recv_sem=recv_hi.at[mask - 1],
            device_id=(flip(my_hi, mask, upper), my_lo),
            device_id_type=pl.DeviceIdType.MESH,
        )

    def chunk_term(chunk, rows, table):
        table = jnp.concatenate([table, table], axis=0)
        product = jnp.dot(split[...], table, preferred_element_type=jnp.float32)
        blocks = [product[p * columns : (p + 1) * columns] for p in range(high)]
        for bit in range(high_bits):
            sign = jnp.broadcast_to(bit_sign(rows, LOW_BITS + bit), (columns, width))
            blocks = [blocks[2 * i] + sign * blocks[2 * i + 1] for i in range(len(blocks) // 2)]
        owner = jnp.bitwise_and(jnp.right_shift(rows, length_bits), device)
        total = blocks[0] * parity_sign(owner, device_bits)
        for unit, mask in enumerate(masks_of(chunk)):
            term[mask] = total[:, unit * group : (unit + 1) * group]

    unrolled = chunks <= 4
    sample_load.wait()
    if unrolled:
        chunk_samples = [chunk_rows(chunk) for chunk in range(chunks)]
        for chunk in range(chunks):
            tables[chunk] = low_table(chunk_samples[chunk])

    sign_load.wait()
    for number in range(LOADS):
        loads[number].wait()
        for block in range(number * high // LOADS, (number + 1) * high // LOADS):
            for half in range(low // LANES):
                lane = block * (low // LANES) + half
                value = design[:, lane * LANES : (lane + 1) * LANES] * signs[
                    lane : lane + 1, :
                ].astype(jnp.float32)
                top = value.astype(jnp.bfloat16)
                rest = (value - top.astype(jnp.float32)).astype(jnp.bfloat16)
                rows = slice(block * columns, (block + 1) * columns)
                split[rows, half * LANES : (half + 1) * LANES] = top
                split[rows, low + half * LANES : low + (half + 1) * LANES] = rest

    if unrolled:
        for chunk in range(chunks):
            chunk_term(chunk, chunk_samples[chunk], tables[chunk])
            if chunk == 0:
                pl.semaphore_wait(barrier, upper + lower - 2)
            for mask in masks_of(chunk):
                if mask > 0:
                    to_hi(mask).start()
    else:
        pl.semaphore_wait(barrier, upper + lower - 2)

        @pl.loop(0, chunks)
        def _(chunk):
            rows = chunk_rows(chunk)
            chunk_term(chunk, rows, low_table(rows))
            for mask in masks_of(chunk):

                @pl.when(mask > 0)
                def _():
                    to_hi(mask).start()

    for mask in range(upper - 1, 0, -1):
        to_hi(mask).wait_recv()
    total = term[0]
    for mask in range(1, upper):
        total = total + landed[mask - 1]
    part[my_lo] = total

    def to_lo(step):
        peer = flip(my_lo, step, lower)
        return pltpu.make_async_remote_copy(
            src_ref=part.at[my_lo],
            dst_ref=part.at[my_lo],
            send_sem=send_lo.at[step - 1],
            recv_sem=recv_lo.at[step - 1],
            device_id=(my_hi, peer),
            device_id_type=pl.DeviceIdType.MESH,
        )

    for step in range(lower - 1, 0, -1):
        to_lo(step).start()
    for step in range(1, lower):
        to_lo(step).wait_recv()
    total = part[0]
    for source in range(1, lower):
        total = total + part[source]
    sampled = total * (1.0 / math.sqrt(length * upper * lower))
    grams[my_hi] = lax.dot_general(
        sampled,
        sampled,
        (((1,), (1,)), ((), ())),
        precision=lax.Precision.HIGHEST,
        preferred_element_type=jnp.float32,
    )

    def to_gram(step):
        peer = flip(my_hi, step, upper)
        return pltpu.make_async_remote_copy(
            src_ref=grams.at[my_hi],
            dst_ref=grams.at[my_hi],
            send_sem=send_gram.at[step - 1],
            recv_sem=recv_gram.at[step - 1],
            device_id=(peer, my_lo),
            device_id_type=pl.DeviceIdType.MESH,
        )

    for step in range(upper - 1, 0, -1):
        to_gram(step).start()
    own = group // lower
    piece = sampled[:, :own]
    for slot in range(1, lower):
        piece = jnp.where(my_lo == slot, sampled[:, slot * own : (slot + 1) * own], piece)
    for step in range(1, upper):
        to_gram(step).wait_recv()
    gram = grams[0]
    for source in range(1, upper):
        gram = gram + grams[source]
    packed_ref[...] = jnp.concatenate(
        [piece, gram * (1.0 / count), jnp.zeros((columns, LANES - own - columns), jnp.float32)],
        axis=1,
    )
    for step in range(1, upper):
        to_hi(step).wait_send()
        to_gram(step).wait_send()
    for step in range(1, lower):
        to_lo(step).wait_send()


def split_kernel(packed_ref, sampled_ref, gram_ref):
    own = sampled_ref.shape[1]
    sampled_ref[...] = packed_ref[:, :own]
    gram_ref[...] = packed_ref[:, own : own + gram_ref.shape[1]]


def on_device(design, signs, samples):
    upper = lax.axis_size("hi")
    lower = lax.axis_size("lo")
    columns, length = design.shape
    count = samples.shape[0]
    group = count // upper
    low = 2**LOW_BITS
    high = length // low
    packed = pl.pallas_call(
        functools.partial(sketch_kernel, (upper, lower, group, length, count)),
        out_shape=jax.ShapeDtypeStruct((columns, LANES), jnp.float32),
        in_specs=[
            pl.BlockSpec(memory_space=pltpu.HBM),
            pl.BlockSpec(memory_space=pltpu.HBM),
            pl.BlockSpec(memory_space=pltpu.HBM),
        ],
        out_specs=pl.BlockSpec(memory_space=pltpu.VMEM),
        scratch_shapes=[
            pltpu.VMEM((columns, length), jnp.float32),
            pltpu.VMEM((length // LANES, LANES), jnp.int32),
            pltpu.VMEM((count // LANES, LANES), jnp.int32),
            pltpu.VMEM((high * columns, 2 * low), jnp.bfloat16),
            pltpu.VMEM((4, low, max(group, 2 * LANES)), jnp.bfloat16),
            pltpu.VMEM((upper, columns, group), jnp.float32),
            pltpu.VMEM((upper - 1, columns, group), jnp.float32),
            pltpu.VMEM((lower, columns, group), jnp.float32),
            pltpu.VMEM((upper, columns, columns), jnp.float32),
            pltpu.SemaphoreType.DMA((LOADS,)),
            pltpu.SemaphoreType.DMA,
            pltpu.SemaphoreType.DMA,
            pltpu.SemaphoreType.DMA((upper - 1,)),
            pltpu.SemaphoreType.DMA((upper - 1,)),
            pltpu.SemaphoreType.DMA((lower - 1,)),
            pltpu.SemaphoreType.DMA((lower - 1,)),
            pltpu.SemaphoreType.DMA((upper - 1,)),
            pltpu.SemaphoreType.DMA((upper - 1,)),
        ],
        compiler_params=pltpu.CompilerParams(
            collective_id=0, has_side_effects=True, vmem_limit_bytes=60 * 2**20
        ),
    )(
        design,
        signs.reshape(length // LANES, LANES),
        samples.reshape(count // LANES, LANES),
    )
    own = group // lower
    return pl.pallas_call(
        split_kernel,
        out_shape=(
            jax.ShapeDtypeStruct((columns, own), jnp.float32),
            jax.ShapeDtypeStruct((columns, columns), jnp.float32),
        ),
        in_specs=[pl.BlockSpec(memory_space=pltpu.VMEM)],
        out_specs=(
            pl.BlockSpec(memory_space=pltpu.VMEM),
            pl.BlockSpec(memory_space=pltpu.VMEM),
        ),
    )(packed)


def solution(mesh):
    placed = (P(None, ("hi", "lo")), P(("hi", "lo")), P())
    return jax.shard_map(
        on_device,
        mesh=mesh,
        in_specs=placed,
        out_specs=(P(None, ("hi", "lo")), P()),
        check_vma=False,
    )
```

```python
import functools
import math

import jax
import jax.numpy as jnp
from jax import lax
from jax.experimental import pallas as pl
from jax.experimental.pallas import tpu as pltpu
from jax.sharding import PartitionSpec as P

LANES = 128
LOW_BITS = 7
LOADS = 2


def bit_sign(values, bit):
    return (1 - 2 * jnp.bitwise_and(jnp.right_shift(values, bit), 1)).astype(jnp.float32)


def parity_sign(values, bits):
    step = 1
    while step < bits:
        values = jnp.bitwise_xor(values, jnp.right_shift(values, step))
        step *= 2
    return bit_sign(values, 0)


def low_table(rows):
    width = rows.shape[1]
    octet = lax.broadcasted_iota(jnp.int32, (8, width), 0)
    table = parity_sign(jnp.bitwise_and(octet, jnp.broadcast_to(rows, (8, width))), 3)
    blocks = [table]
    for bit in range(3, LOW_BITS):
        sign = jnp.broadcast_to(bit_sign(rows, bit), (8, width))
        blocks = blocks + [block * sign for block in blocks]
    return jnp.concatenate(blocks, axis=0).astype(jnp.bfloat16)


def flip(index, mask, size):
    result = 0
    bit = 1
    while bit < size:
        result = result + bit * lax.rem(lax.div(index, bit) + lax.div(mask, bit), 2)
        bit *= 2
    return result


def sketch_kernel(
    sizes,
    design_hbm,
    signs_hbm,
    samples_hbm,
    packed_ref,
    design,
    signs,
    samples_ref,
    split,
    tables,
    term,
    landed,
    part,
    grams,
    load_sem,
    sign_sem,
    sample_sem,
    send_hi,
    recv_hi,
    send_lo,
    recv_lo,
    send_gram,
    recv_gram,
):
    upper, lower, group, length, count = sizes
    columns = design.shape[0]
    low = 2**LOW_BITS
    high = length // low
    high_bits = high.bit_length() - 1
    length_bits = length.bit_length() - 1
    device_bits = (upper * lower).bit_length() - 1
    my_hi = lax.axis_index("hi")
    my_lo = lax.axis_index("lo")
    device = my_hi * lower + my_lo

    sample_load = pltpu.make_async_copy(samples_hbm, samples_ref, sample_sem)
    sample_load.start()
    sign_load = pltpu.make_async_copy(signs_hbm, signs, sign_sem)
    sign_load.start()
    piece = length // LOADS
    loads = []
    for number in range(LOADS):
        here = pl.ds(number * piece, piece)
        loads.append(
            pltpu.make_async_copy(design_hbm.at[:, here], design.at[:, here], load_sem.at[number])
        )
        loads[-1].start()

    barrier = pltpu.get_barrier_semaphore()
    for step in range(upper - 1, 0, -1):
        peer = flip(my_hi, step, upper)
        pl.semaphore_signal(
            barrier, inc=1, device_id=(peer, my_lo), device_id_type=pl.DeviceIdType.MESH
        )
    for step in range(lower - 1, 0, -1):
        peer = flip(my_lo, step, lower)
        pl.semaphore_signal(
            barrier, inc=1, device_id=(my_hi, peer), device_id_type=pl.DeviceIdType.MESH
        )

    tiles = group // LANES
    per_chunk = max(1, 2 // tiles)
    chunks = upper // per_chunk
    width = per_chunk * group

    def masks_of(chunk):
        return [upper - 1 - chunk * per_chunk - unit for unit in range(per_chunk)]

    def chunk_rows(chunk):
        rows = []
        for mask in masks_of(chunk):
            target = flip(my_hi, mask, upper)
            for tile in range(tiles):
                rows.append(samples_ref[pl.ds(target * tiles + tile, 1), :])
        return jnp.concatenate(rows, axis=1)

    def to_hi(mask):
        return pltpu.make_async_remote_copy(
            src_ref=term.at[mask],
            dst_ref=landed.at[mask - 1],
            send_sem=send_hi.at[mask - 1],
            recv_sem=recv_hi.at[mask - 1],
            device_id=(flip(my_hi, mask, upper), my_lo),
            device_id_type=pl.DeviceIdType.MESH,
        )

    def chunk_term(chunk, rows, table):
        table = jnp.concatenate([table, table], axis=0)
        product = jnp.dot(split[...], table, preferred_element_type=jnp.float32)
        blocks = [product[p * columns : (p + 1) * columns] for p in range(high)]
        for bit in range(high_bits):
            sign = jnp.broadcast_to(bit_sign(rows, LOW_BITS + bit), (columns, width))
            blocks = [blocks[2 * i] + sign * blocks[2 * i + 1] for i in range(len(blocks) // 2)]
        owner = jnp.bitwise_and(jnp.right_shift(rows, length_bits), device)
        total = blocks[0] * parity_sign(owner, device_bits)
        for unit, mask in enumerate(masks_of(chunk)):
            term[mask] = total[:, unit * group : (unit + 1) * group]

    unrolled = chunks <= 4
    sample_load.wait()
    if unrolled:
        chunk_samples = [chunk_rows(chunk) for chunk in range(chunks)]
        for chunk in range(chunks):
            tables[chunk] = low_table(chunk_samples[chunk])

    sign_load.wait()
    for number in range(LOADS):
        loads[number].wait()
        for block in range(number * high // LOADS, (number + 1) * high // LOADS):
            for half in range(low // LANES):
                lane = block * (low // LANES) + half
                value = design[:, lane * LANES : (lane + 1) * LANES] * signs[
                    lane : lane + 1, :
                ].astype(jnp.float32)
                top = value.astype(jnp.bfloat16)
                rest = (value - top.astype(jnp.float32)).astype(jnp.bfloat16)
                rows = slice(block * columns, (block + 1) * columns)
                split[rows, half * LANES : (half + 1) * LANES] = top
                split[rows, low + half * LANES : low + (half + 1) * LANES] = rest

    if unrolled:
        for chunk in range(chunks):
            chunk_term(chunk, chunk_samples[chunk], tables[chunk])
            if chunk == 0:
                pl.semaphore_wait(barrier, upper + lower - 2)
            for mask in masks_of(chunk):
                if mask > 0:
                    to_hi(mask).start()
    else:
        pl.semaphore_wait(barrier, upper + lower - 2)

        @pl.loop(0, chunks)
        def _(chunk):
            rows = chunk_rows(chunk)
            chunk_term(chunk, rows, low_table(rows))
            for mask in masks_of(chunk):

                @pl.when(mask > 0)
                def _():
                    to_hi(mask).start()

    for mask in range(upper - 1, 0, -1):
        to_hi(mask).wait_recv()
    total = term[0]
    for mask in range(1, upper):
        total = total + landed[mask - 1]
    part[my_lo] = total

    def to_lo(step):
        peer = flip(my_lo, step, lower)
        return pltpu.make_async_remote_copy(
            src_ref=part.at[my_lo],
            dst_ref=part.at[my_lo],
            send_sem=send_lo.at[step - 1],
            recv_sem=recv_lo.at[step - 1],
            device_id=(my_hi, peer),
            device_id_type=pl.DeviceIdType.MESH,
        )

    for step in range(lower - 1, 0, -1):
        to_lo(step).start()
    for step in range(1, lower):
        to_lo(step).wait_recv()
    total = part[0]
    for source in range(1, lower):
        total = total + part[source]
    sampled = total * (1.0 / math.sqrt(length * upper * lower))
    gram = lax.dot_general(
        sampled,
        sampled,
        (((1,), (1,)), ((), ())),
        precision=lax.Precision.HIGHEST,
        preferred_element_type=jnp.float32,
    )
    grams[my_hi] = jnp.concatenate(
        [gram, jnp.zeros((columns, LANES - columns), jnp.float32)], axis=1
    )

    def to_gram(step):
        peer = flip(my_hi, step, upper)
        return pltpu.make_async_remote_copy(
            src_ref=grams.at[my_hi],
            dst_ref=grams.at[my_hi],
            send_sem=send_gram.at[step - 1],
            recv_sem=recv_gram.at[step - 1],
            device_id=(peer, my_lo),
            device_id_type=pl.DeviceIdType.MESH,
        )

    for step in range(upper - 1, 0, -1):
        to_gram(step).start()
    own = group // lower
    piece = sampled[:, :own]
    for slot in range(1, lower):
        piece = jnp.where(my_lo == slot, sampled[:, slot * own : (slot + 1) * own], piece)
    for step in range(1, upper):
        to_gram(step).wait_recv()
    gram = grams[0]
    for source in range(1, upper):
        gram = gram + grams[source]
    packed_ref[...] = jnp.concatenate(
        [piece, gram[:, :columns] * (1.0 / count), jnp.zeros((columns, LANES - own - columns), jnp.float32)],
        axis=1,
    )
    for step in range(1, upper):
        to_hi(step).wait_send()
        to_gram(step).wait_send()
    for step in range(1, lower):
        to_lo(step).wait_send()


def split_kernel(packed_ref, sampled_ref, gram_ref):
    own = sampled_ref.shape[1]
    sampled_ref[...] = packed_ref[:, :own]
    gram_ref[...] = packed_ref[:, own : own + gram_ref.shape[1]]


def on_device(design, signs, samples):
    upper = lax.axis_size("hi")
    lower = lax.axis_size("lo")
    columns, length = design.shape
    count = samples.shape[0]
    group = count // upper
    low = 2**LOW_BITS
    high = length // low
    packed = pl.pallas_call(
        functools.partial(sketch_kernel, (upper, lower, group, length, count)),
        out_shape=jax.ShapeDtypeStruct((columns, LANES), jnp.float32),
        in_specs=[
            pl.BlockSpec(memory_space=pltpu.HBM),
            pl.BlockSpec(memory_space=pltpu.HBM),
            pl.BlockSpec(memory_space=pltpu.HBM),
        ],
        out_specs=pl.BlockSpec(memory_space=pltpu.VMEM),
        scratch_shapes=[
            pltpu.VMEM((columns, length), jnp.float32),
            pltpu.VMEM((length // LANES, LANES), jnp.int32),
            pltpu.VMEM((count // LANES, LANES), jnp.int32),
            pltpu.VMEM((high * columns, 2 * low), jnp.bfloat16),
            pltpu.VMEM((4, low, max(group, 2 * LANES)), jnp.bfloat16),
            pltpu.VMEM((upper, columns, group), jnp.float32),
            pltpu.VMEM((upper - 1, columns, group), jnp.float32),
            pltpu.VMEM((lower, columns, group), jnp.float32),
            pltpu.VMEM((upper, columns, LANES), jnp.float32),
            pltpu.SemaphoreType.DMA((LOADS,)),
            pltpu.SemaphoreType.DMA,
            pltpu.SemaphoreType.DMA,
            pltpu.SemaphoreType.DMA((upper - 1,)),
            pltpu.SemaphoreType.DMA((upper - 1,)),
            pltpu.SemaphoreType.DMA((lower - 1,)),
            pltpu.SemaphoreType.DMA((lower - 1,)),
            pltpu.SemaphoreType.DMA((upper - 1,)),
            pltpu.SemaphoreType.DMA((upper - 1,)),
        ],
        compiler_params=pltpu.CompilerParams(
            collective_id=0, has_side_effects=True, vmem_limit_bytes=60 * 2**20
        ),
    )(
        design,
        signs.reshape(length // LANES, LANES),
        samples.reshape(count // LANES, LANES),
    )
    own = group // lower
    return pl.pallas_call(
        split_kernel,
        out_shape=(
            jax.ShapeDtypeStruct((columns, own), jnp.float32),
            jax.ShapeDtypeStruct((columns, columns), jnp.float32),
        ),
        in_specs=[pl.BlockSpec(memory_space=pltpu.VMEM)],
        out_specs=(
            pl.BlockSpec(memory_space=pltpu.VMEM),
            pl.BlockSpec(memory_space=pltpu.VMEM),
        ),
    )(packed)


def solution(mesh):
    placed = (P(None, ("hi", "lo")), P(("hi", "lo")), P())
    return jax.shard_map(
        on_device,
        mesh=mesh,
        in_specs=placed,
        out_specs=(P(None, ("hi", "lo")), P()),
        check_vma=False,
    )
```
